256 devices in a mesh: row: 32 (over y, z), ka: 8 (over x, core).
Axes of the slice: x: 4, y: 4, z: 8, core: 2. Of those that a mesh axis runs over, the one named last changes fastest.
Arguments:
- pair_table: int32 [8], replicated, may hold values from 0 to 7, as said below
- cholesky: bfloat16 [8, 3000, 3072], P('ka', None, 'row'), may hold values from -0.875 to 0.875
- amplitudes: bfloat16 [8, 3072, 3072], P('ka', 'row'), may hold values from -0.109375 to 0.109375
- denominators: float32 [8, 3072, 3072], P('ka', 'row'), may hold values from 1 to 6
Outputs:
- new_amplitudes: bfloat16 [8, 3072, 3072], P('ka', 'row')
The draws below stay inside these ranges and needn't reach their ends.
Inputs may be any that keep to these rules, and one draw needn't show every extreme that they name: `pair_table`: blocks may couple to any block, to themselves too, and several blocks may couple to the same one.
All inputs are finite; a program needn't handle non-finite values.
Results may differ from the reference program's by a relative error of at most 0.0046.
Values may be sent and summed in bfloat16 or wider, within the bound.
No kernel may reach another device: no remote copies, remote signals or barrier semaphores. Data moves between devices by JAX's collectives and lax.ppermute only.
A program may use at most 192 MiB of HBM per device.

```python
import math
import jax
import jax.numpy as jnp
from jax import lax

NAUX = 3000
NK = 8
OV = 3072


def draw_pair_table(key, part):
    key = jax.random.fold_in(key, 11)
    base_key, pick_key, step_key = jax.random.split(key, 3)
    table = jax.random.randint(base_key, (NK,), 0, NK, dtype=jnp.int32)
    first = jax.random.randint(pick_key, (), 0, NK, dtype=jnp.int32)
    offset = jax.random.randint(step_key, (), 1, NK, dtype=jnp.int32)
    second = (first + offset) % NK
    places = jnp.arange(NK, dtype=jnp.int32)
    table = jnp.where(places == first, NK - 1, table)
    table = jnp.where(places == second, 0, table)
    return table.astype(jnp.int32)


def block_scale(key, shape, cuts, low, top_value):
    def one(axis_at, parts):
        draws = jax.random.uniform(jax.random.fold_in(jax.random.fold_in(key, 6), axis_at), (parts,), jnp.float32, low / len(cuts), top_value / len(cuts))
        return jnp.repeat(jnp.exp(draws), shape[axis_at] // parts).reshape((-1,) + (1,) * (len(shape) - axis_at - 1))

    gain = one(*cuts[0])
    for cut in cuts[1:]:
        gain = gain * one(*cut)
    return gain


def normal_values(rng, shape, width, reach, cuts=(), kind=jnp.bfloat16):
    values = width * jax.random.normal(rng, shape, jnp.float32)
    if cuts:
        values = values * block_scale(rng, shape, cuts, -0.22, 0.18)
    return jnp.clip(values, -reach, reach).astype(kind)


def setup_inputs(seed: int = 0) -> dict:
    seeds = jax.random.split(jax.random.key(seed), 5)
    pair_table = draw_pair_table(jax.random.fold_in(seeds[4], 71), 0)
    cholesky = normal_values(seeds[1], (NK, NAUX, OV), (NAUX ** 0.5) ** -0.5, 0.875, ((0, 8), (2, 32)))
    amplitudes = normal_values(seeds[2], (NK, OV, OV), OV ** -0.5, 0.109375, ((0, 8), (1, 32)))
    denominators = jnp.clip(jnp.exp(math.log(6.0) - 1.7917595 * jax.random.uniform(seeds[3], (NK, OV, OV), jnp.float32) ** block_scale(seeds[3], (NK, OV, OV), ((0, 8), (1, 32)), -0.2, 0.2)), 1.0, 6.0)
    return {"pair_table": pair_table, "cholesky": cholesky, "amplitudes": amplitudes, "denominators": denominators}


def one_block(args):
    chol, amps, denom = args
    cholf = chol.astype(jnp.float32)
    tx = lax.dot_general(amps, chol, (((1,), (1,)), ((), ())), preferred_element_type=jnp.float32)
    left = (jnp.transpose(cholf) + tx).astype(jnp.bfloat16)
    cycle = jnp.dot(chol, amps, preferred_element_type=jnp.float32)
    right = (cholf + cycle).astype(jnp.bfloat16)
    prod = jnp.dot(left, right, preferred_element_type=jnp.float32)
    return (-prod / denom).astype(jnp.bfloat16)


def reference(pair_table, cholesky, amplitudes, denominators):
    chosen = cholesky[pair_table.astype(jnp.int32)]
    return lax.map(one_block, (chosen, amplitudes, denominators))
```

```python
import jax
import jax.numpy as jnp
from jax import lax
from jax.sharding import Mesh
from jax.sharding import PartitionSpec as P

NY, NZ, NX, NC = 4, 8, 4, 2
BF, F32 = jnp.bfloat16, jnp.float32
SIZES = {"y": NY, "z": NZ, "x": NX, "c": NC}


def shift(block, axis, step):
    n = SIZES[axis]
    return lax.ppermute(block, axis, [(i, (i + step) % n) for i in range(n)])


def pick(blocks, index):
    return lax.select_n(index, *blocks)


def halves(block):
    h = block.shape[0] // 2
    return block[:h], block[h:]


def shards(pair_table, cholesky, amplitudes, denominators):
    y, x, c = lax.axis_index("y"), lax.axis_index("x"), lax.axis_index("c")
    q = x * NC + c
    amps = amplitudes[0]
    pairs, naux = amps.shape[0], cholesky.shape[1]
    aux = -(-naux // (128 * NY)) * 128
    width = NZ * pairs

    amps_i = lax.all_gather(amps, "z", axis=0, tiled=True)
    amps_j = lax.all_gather(amps, "y", axis=0, tiled=True)

    own = jnp.pad(jnp.transpose(cholesky[0]), ((0, 0), (0, NY * aux - naux)))
    slices = jnp.transpose(own.reshape(pairs, NY, aux), (1, 0, 2))
    mine = lax.all_to_all(slices, "y", split_axis=0, concat_axis=0, tiled=True).reshape(NY * pairs, aux)

    fore, back = shift(mine, "x", 1), shift(mine, "x", -1)
    low, high = halves(fore)[0], halves(back)[1]
    far = jnp.concatenate([shift(low, "x", 1), shift(high, "x", -1)], axis=0)
    blocks = [mine, back, far, fore]
    wanted, theirs = pair_table[q], pair_table[q + 1 - 2 * c]
    sent = shift(pick(blocks, (theirs // NC - x) % NX), "c", 1)
    chosen = jnp.where(wanted % NC == c, pick(blocks, (wanted // NC - x) % NX), sent)

    full = lax.all_gather(chosen.reshape(NY, pairs, aux), "z", axis=1, tiled=False)
    full = full.reshape(NY * width, aux)

    left = (chosen.astype(F32) + jnp.dot(amps_j, full, preferred_element_type=F32)).astype(BF)
    part = [
        lax.dot_general(left, full[i * width : (i + 1) * width], (((1,), (1,)), ((), ())), preferred_element_type=F32).astype(BF)
        for i in range(NY)
    ]
    part = lax.all_to_all(jnp.stack(part), "y", split_axis=0, concat_axis=0, tiled=True)
    total = jnp.sum(part.astype(F32), axis=0)
    prod = jnp.dot(total.astype(BF), amps_i, preferred_element_type=F32)
    place = lax.dynamic_update_slice(jnp.zeros_like(prod), total, (0, y * width))
    prod = (prod + place).astype(BF).reshape(NY, pairs, NY * width)
    prod = lax.all_to_all(prod, "y", split_axis=0, concat_axis=0, tiled=True)
    return (-jnp.sum(prod.astype(F32), axis=0) / denominators[0]).astype(BF)[None]


def solution(mesh):
    grid = Mesh(mesh.devices.reshape(NY, NZ, NX, NC), ("y", "z", "x", "c"))
    ka, row = ("x", "c"), ("y", "z")
    in_specs = (P(), P(ka, None, row), P(ka, row, None), P(ka, row, None))
    return jax.shard_map(shards, mesh=grid, in_specs=in_specs, out_specs=P(ka, row, None), check_vma=False)
```

```python
import functools

import jax
import jax.numpy as jnp
from jax import lax
from jax.experimental import pallas as pl
from jax.experimental.pallas import tpu as pltpu
from jax.sharding import Mesh
from jax.sharding import PartitionSpec as P

NY, NZ, NX, NC = 4, 8, 4, 2
BF, F32 = jnp.bfloat16, jnp.float32
SIZES = {"y": NY, "z": NZ, "x": NX, "c": NC}
ANY = pl.BlockSpec(memory_space=pl.ANY)
VMEM = pl.BlockSpec(memory_space=pltpu.VMEM)
SMEM = pl.BlockSpec(memory_space=pltpu.SMEM)


def params(mib):
    return pltpu.CompilerParams(vmem_limit_bytes=mib * 2**20)


def shift(block, axis, step):
    n = SIZES[axis]
    with jax.named_scope(f"{axis}{step}_{block.size * 2 // 1000}kB"):
        return lax.ppermute(block, axis, [(i, (i + step) % n) for i in range(n)])


def dot(a, b):
    return jnp.dot(a, b, preferred_element_type=F32)


def dot_t(a, b):
    return lax.dot_general(a, b, (((1,), (1,)), ((), ())), preferred_element_type=F32)


def cost(flops):
    return pl.CostEstimate(flops=flops, bytes_accessed=8 * 2**20, transcendentals=0)


def swap_kernel(place_ref, table_ref, held_ref, sent_ref, sems):
    c = place_ref[2]
    copies = []
    for k in range(NX):
        want = table_ref[k * NC + 1 - c]
        copies.append(pltpu.make_async_copy(held_ref.at[want >> 1], sent_ref.at[k], sems.at[k]))
        copies[-1].start()
    for copy in copies:
        copy.wait()


def mine_kernel(place_ref, table_ref, held_ref, sent_ref, amps_ref, mine_ref, out_ref, sems):
    c = place_ref[2]
    amps = pltpu.make_async_copy(amps_ref, out_ref, sems.at[NX])
    amps.start()
    for k in range(NX):
        want = table_ref[k * NC + c]
        here = (want & 1) == c

        @pl.when(here)
        def _():
            pltpu.make_async_copy(held_ref.at[want >> 1], mine_ref.at[k], sems.at[k]).start()

        @pl.when(jnp.logical_not(here))
        def _():
            pltpu.make_async_copy(sent_ref.at[k], mine_ref.at[k], sems.at[k]).start()

    for k in range(NX):
        pltpu.make_async_copy(sent_ref.at[k], mine_ref.at[k], sems.at[k]).wait()
    amps.wait()


def choose(kernel, results, place, table, *arrays):
    return pl.pallas_call(
        kernel,
        out_shape=[jax.ShapeDtypeStruct(a.shape, a.dtype) for a in results],
        in_specs=[SMEM, SMEM] + [ANY] * len(arrays),
        out_specs=[ANY] * len(results),
        scratch_shapes=[pltpu.SemaphoreType.DMA((NX + 1,))],
        compiler_params=params(2),
    )(place, table, *arrays)


def join_kernel(parts_ref, first_ref, chosen_ref, sems):
    copies = [pltpu.make_async_copy(parts_ref.at[k], chosen_ref.at[:, k], sems.at[k]) for k in range(NX)]
    for copy in copies:
        copy.start()
    for copy in copies:
        copy.wait()


def join(parts, first):
    nx, ny, third, aux = parts.shape
    return pl.pallas_call(
        join_kernel,
        out_shape=jax.ShapeDtypeStruct((ny, nx, third, aux), BF),
        in_specs=[ANY] * 2,
        out_specs=ANY,
        scratch_shapes=[pltpu.SemaphoreType.DMA((NX,))],
        compiler_params=params(2),
    )(parts, first)


def left_kernel(dist, place_ref, amps_ref, *refs):
    blocks, (left_ref, full_ref, sems) = refs[:-3], refs[-3:]
    z, rows = place_ref[1], blocks[0].shape[0]
    copies = []
    for n, d in enumerate(dist):
        copies.append(pltpu.make_async_copy(blocks[n], full_ref.at[(z + NZ + d) % NZ], sems.at[n]))
        copies[-1].start()
    for n, d in enumerate(dist):
        at = (z + NZ + d) % NZ
        copies[n].wait()
        block = full_ref[at]
        part = dot(amps_ref[:, pl.ds(pl.multiple_of(at * rows, 128), rows)], block)
        if n:
            left_ref[...] += part
        else:
            left_ref[...] = block.astype(F32) + part


def partial_kernel(pairs, place_ref, amps_ref, left_ref, full_ref, far_a_ref, far_b_ref, late_ref, own_ref, *refs):
    send_refs, (later_ref, left, sem) = refs[:-3], refs[-3:]
    later = pltpu.make_async_copy(late_ref, later_ref, sem)
    later.start()
    y, z, rows = place_ref[0], place_ref[1], left_ref.shape[0]
    last = (z + NZ // 2) % NZ
    amps = amps_ref[:, pl.ds(pl.multiple_of(last * rows, 128), rows)]
    h = far_a_ref.shape[1]
    for at, far in ((0, far_a_ref), (h, far_b_ref)):
        cols = pl.ds(at, h)
        left[:, cols] = (left_ref[:, cols] + dot(amps, far[...])).astype(BF)
    for n, d in enumerate((2, 1, 3, 0)):
        at = pl.ds(pl.multiple_of((y + d) % NY * pairs, 32), pairs)
        far = jnp.concatenate([far_a_ref[at], far_b_ref[at]], axis=1)
        block = jnp.concatenate([jnp.where(last == k, far, full_ref[k, at]) for k in range(NZ)], axis=0)
        part = dot_t(left[...], block)
        if d:
            send_refs[n][...] = part.astype(BF)
        else:
            own_ref[...] = part
    later.wait()


def out_kernel(pairs, first, place_ref, total_ref, amps_ref, own_ref, *refs):
    send_refs, (total, rows, amps, sems) = refs[:-4], refs[-4:]
    y = place_ref[0]
    width = total_ref.shape[1]
    step = amps.shape[2]
    copies = [
        pltpu.make_async_copy(amps_ref.at[:, pl.ds(k * step, step)], amps.at[k], sems.at[k])
        for k in range(amps.shape[0])
    ]
    for copy in copies:
        copy.start()
    for d in range(NY):
        block = total_ref[pl.ds(pl.multiple_of((y + d) % NY * pairs, 32), pairs)]
        total[d * pairs : (d + 1) * pairs] = block
        rows[d * pairs : (d + 1) * pairs] = block.astype(BF)
    for k, copy in enumerate(copies):
        n, part = divmod(first + k * step, width)
        cols = pl.ds(k * step, step)
        copy.wait()
        prod = dot(rows[...], amps[k])
        prod += jnp.where(y == n, total[:, part : part + step], 0.0)
        own_ref[:, cols] = prod[:pairs]
        for d in range(1, NY):
            send_refs[d - 1][:, cols] = prod[d * pairs : (d + 1) * pairs].astype(BF)


def out_products(place, total, amps_i, first, pairs):
    rows, cols = amps_i.shape
    step = total.shape[1] // 2
    return pl.pallas_call(
        functools.partial(out_kernel, pairs, first),
        out_shape=[jax.ShapeDtypeStruct((pairs, cols), F32)] + [jax.ShapeDtypeStruct((pairs, cols), BF)] * (NY - 1),
        in_specs=[SMEM, VMEM, ANY],
        out_specs=[VMEM] * NY,
        scratch_shapes=[
            pltpu.VMEM(total.shape, F32),
            pltpu.VMEM(total.shape, BF),
            pltpu.VMEM((cols // step, rows, step), BF),
            pltpu.SemaphoreType.DMA((cols // step,)),
        ],
        compiler_params=params(10),
        cost_estimate=cost(2 * total.size * cols),
    )(place, total, amps_i)


def shards(pair_table, cholesky, amplitudes, denominators):
    y, z, x, c = (lax.axis_index(a) for a in ("y", "z", "x", "c"))
    place = jnp.stack([y, z, c])
    amps = amplitudes[0]
    pairs, naux = amps.shape[0], cholesky.shape[1]
    aux = -(-naux // (128 * NY)) * 128
    width = NZ * pairs
    rows = NY * pairs
    third = pairs // NX

    early = 4 * NY * width // 8
    amps_i0 = lax.all_gather(amps[:, :early], "z", axis=0, tiled=True)
    by_z = jnp.transpose(amps.reshape(pairs, NY, NZ, pairs), (0, 2, 1, 3)).reshape(pairs, NY * width)

    own = jnp.pad(jnp.transpose(cholesky[0]), ((0, 0), (0, NY * aux - naux)))
    own = jnp.transpose(own.reshape(NX, third, NY, aux), (0, 2, 1, 3)).reshape(NX * NY, third, aux)
    held = lax.all_to_all(own, ("x", "y"), split_axis=0, concat_axis=0, tiled=True).reshape(NX, NY, third, aux)
    (sent,) = choose(swap_kernel, (held,), place, pair_table, held)
    mine, by_z = choose(mine_kernel, (held, by_z), place, pair_table, held, shift(sent, "c", 1), by_z)
    amps_j = lax.all_gather(by_z, "y", axis=0, tiled=True)
    parts = lax.all_to_all(mine, "x", split_axis=0, concat_axis=0, tiled=True)
    chosen = join(parts, amps_i0).reshape(rows, aux)

    dist, blocks = [0], [chosen]
    fore = back = chosen
    for s in range(1, NZ // 2):
        fore, back = shift(fore, "z", 1), shift(back, "z", -1)
        dist += [-s, s]
        blocks += [fore, back]
    h = aux // 2
    far_a, far_b = shift(fore[:, :h], "z", 1), shift(back[:, h:], "z", -1)

    left, full = pl.pallas_call(
        functools.partial(left_kernel, dist),
        out_shape=[
            jax.ShapeDtypeStruct((rows, aux), F32),
            jax.ShapeDtypeStruct((NZ, rows, aux), BF),
        ],
        in_specs=[SMEM, VMEM] + [ANY] * len(blocks),
        out_specs=[VMEM] * 2,
        scratch_shapes=[pltpu.SemaphoreType.DMA((len(blocks),))],
        compiler_params=params(8),
        cost_estimate=cost(2 * rows * aux * rows * len(blocks)),
    )(place, amps_j, *blocks)
    late = amps[:, early:]
    total, *send, later = pl.pallas_call(
        functools.partial(partial_kernel, pairs),
        out_shape=[jax.ShapeDtypeStruct((rows, width), F32)] + [jax.ShapeDtypeStruct((rows, width), BF)] * (NY - 1)
        + [jax.ShapeDtypeStruct(late.shape, BF)],
        in_specs=[SMEM] + [VMEM] * 5 + [ANY],
        out_specs=[VMEM] * NY + [ANY],
        scratch_shapes=[pltpu.VMEM((rows, aux), BF), pltpu.SemaphoreType.DMA],
        compiler_params=params(8),
        cost_estimate=cost(2 * rows * aux * (rows + NY * width)),
    )(place, amps_j, left, full, far_a, far_b, late)
    amps_i1 = lax.all_gather(later, "z", axis=0, tiled=True)
    parts = [shift(part, "y", d) for part, d in zip(send, (2, 1, 3))]
    for part in parts:
        total = total + part.astype(F32)

    outs = []
    for first, amps_i in ((0, amps_i0), (early, amps_i1)):
        out, *send = out_products(place, total, amps_i, first, pairs)
        for d in (2, 1, 3):
            out = out + shift(send[d - 1], "y", d).astype(F32)
        outs.append(out)
    return (-jnp.concatenate(outs, axis=1) / denominators[0]).astype(BF)[None]


def solution(mesh):
    grid = Mesh(mesh.devices.reshape(NY, NZ, NX, NC), ("y", "z", "x", "c"))
    ka, row = ("x", "c"), ("y", "z")
    in_specs = (P(), P(ka, None, row), P(ka, row, None), P(ka, row, None))
    return jax.shard_map(shards, mesh=grid, in_specs=in_specs, out_specs=P(ka, row, None), check_vma=False)
```

```python
import functools

import jax
import jax.numpy as jnp
from jax import lax
from jax.experimental import pallas as pl
from jax.experimental.pallas import tpu as pltpu
from jax.sharding import Mesh
from jax.sharding import PartitionSpec as P

NY, NZ, NX, NC = 4, 8, 4, 2
BF, F32 = jnp.bfloat16, jnp.float32
SIZES = {"y": NY, "z": NZ, "x": NX, "c": NC}
ANY = pl.BlockSpec(memory_space=pl.ANY)
VMEM = pl.BlockSpec(memory_space=pltpu.VMEM)
SMEM = pl.BlockSpec(memory_space=pltpu.SMEM)


def params(mib):
    return pltpu.CompilerParams(vmem_limit_bytes=mib * 2**20)


def shift(block, axis, step):
    n = SIZES[axis]
    with jax.named_scope(f"{axis}{step}_{block.size * 2 // 1000}kB"):
        return lax.ppermute(block, axis, [(i, (i + step) % n) for i in range(n)])


def dot(a, b):
    return jnp.dot(a, b, preferred_element_type=F32)


def dot_t(a, b):
    return lax.dot_general(a, b, (((1,), (1,)), ((), ())), preferred_element_type=F32)


def cost(flops):
    return pl.CostEstimate(flops=flops, bytes_accessed=8 * 2**20, transcendentals=0)


def swap_kernel(place_ref, table_ref, held_ref, amps_ref, sent_ref, out_ref, sems):
    c = place_ref[2]
    copies = [pltpu.make_async_copy(amps_ref, out_ref, sems.at[NX])]
    copies[0].start()
    for k in range(NX):
        want = table_ref[k * NC + 1 - c]
        copies.append(pltpu.make_async_copy(held_ref.at[want >> 1], sent_ref.at[k], sems.at[k]))
        copies[-1].start()
    for copy in copies:
        copy.wait()


def mine_kernel(place_ref, table_ref, held_ref, sent_ref, mine_ref, sems):
    c = place_ref[2]
    for k in range(NX):
        want = table_ref[k * NC + c]
        here = (want & 1) == c

        @pl.when(here)
        def _():
            pltpu.make_async_copy(held_ref.at[want >> 1], mine_ref.at[k], sems.at[k]).start()

        @pl.when(jnp.logical_not(here))
        def _():
            pltpu.make_async_copy(sent_ref.at[k], mine_ref.at[k], sems.at[k]).start()

    for k in range(NX):
        pltpu.make_async_copy(sent_ref.at[k], mine_ref.at[k], sems.at[k]).wait()


def choose(kernel, results, place, table, *arrays):
    return pl.pallas_call(
        kernel,
        out_shape=[jax.ShapeDtypeStruct(a.shape, a.dtype) for a in results],
        in_specs=[SMEM, SMEM] + [ANY] * len(arrays),
        out_specs=[ANY] * len(results),
        scratch_shapes=[pltpu.SemaphoreType.DMA((NX + 1,))],
        compiler_params=params(2),
    )(place, table, *arrays)


def join_kernel(parts_ref, first_ref, chosen_ref, sems):
    copies = [pltpu.make_async_copy(parts_ref.at[k], chosen_ref.at[:, k], sems.at[k]) for k in range(NX)]
    for copy in copies:
        copy.start()
    for copy in copies:
        copy.wait()


def join(parts, first):
    nx, ny, third, aux = parts.shape
    return pl.pallas_call(
        join_kernel,
        out_shape=jax.ShapeDtypeStruct((ny, nx, third, aux), BF),
        in_specs=[ANY] * 2,
        out_specs=ANY,
        scratch_shapes=[pltpu.SemaphoreType.DMA((NX,))],
        compiler_params=params(2),
    )(parts, first)


def last_kernel(fore_ref, back_ref, late_ref, a_ref, b_ref, later_ref, sems):
    h = a_ref.shape[1]
    copies = [
        pltpu.make_async_copy(fore_ref.at[:, pl.ds(0, h)], a_ref, sems.at[0]),
        pltpu.make_async_copy(back_ref.at[:, pl.ds(h, h)], b_ref, sems.at[1]),
        pltpu.make_async_copy(late_ref, later_ref, sems.at[2]),
    ]
    for copy in copies:
        copy.start()
    for copy in copies:
        copy.wait()


def last_step(fore, back, late):
    rows, aux = fore.shape
    half = jax.ShapeDtypeStruct((rows, aux // 2), BF)
    return pl.pallas_call(
        last_kernel,
        out_shape=[half, half, jax.ShapeDtypeStruct(late.shape, BF)],
        in_specs=[ANY] * 3,
        out_specs=[ANY] * 3,
        scratch_shapes=[pltpu.SemaphoreType.DMA((3,))],
        compiler_params=params(2),
    )(fore, back, late)


def left_kernel(dist, more, place_ref, amps_ref, *refs):
    blocks, refs = refs[: len(dist)], refs[len(dist) :]
    before, (left_ref, full_ref, *last_ref, amps, sems) = (refs[:2], refs[2:]) if more else (None, refs)
    z, rows = place_ref[1], blocks[0].shape[0]

    def columns(d):
        return pl.ds(pl.multiple_of((z + NZ + d) % NZ * rows, 128), rows)

    copies = []
    for n, d in enumerate(dist):
        copies.append(pltpu.make_async_copy(blocks[n], full_ref.at[(z + NZ + d) % NZ], sems.at[n, 0]))
        copies.append(pltpu.make_async_copy(amps_ref.at[:, columns(d)], amps.at[n], sems.at[n, 1]))
    if more:
        copies.append(pltpu.make_async_copy(amps_ref.at[:, columns(NZ // 2)], last_ref[0], sems.at[len(dist), 0]))
    for copy in copies:
        copy.start()
    for n, d in enumerate(dist):
        copies[2 * n].wait()
        copies[2 * n + 1].wait()
        block = full_ref[(z + NZ + d) % NZ]
        part = dot(amps[n], block)
        if n:
            left_ref[...] += part
        elif more:
            left_ref[...] = before[0][...] + part
        else:
            left_ref[...] = block.astype(F32) + part
    if more:
        copies[-1].wait()


def add_left(place, amps, dist, blocks, before=()):
    rows, aux = blocks[0].shape
    n, more = len(dist), bool(before)
    shapes = [((rows, aux), F32), ((NZ, rows, aux), BF)] + [((rows, rows), BF)] * more
    return pl.pallas_call(
        functools.partial(left_kernel, dist, more),
        out_shape=[jax.ShapeDtypeStruct(*a) for a in shapes],
        in_specs=[SMEM, VMEM] + [ANY] * n + [VMEM] * len(before),
        out_specs=[VMEM] * len(shapes),
        scratch_shapes=[pltpu.VMEM((n, rows, rows), BF), pltpu.SemaphoreType.DMA((n + 1, 2))],
        input_output_aliases={2 + n: 0, 3 + n: 1} if more else {},
        compiler_params=params(8),
        cost_estimate=cost(2 * rows * aux * rows * n),
    )(place, amps, *blocks, *before)


def first_kernel(pairs, place_ref, amps_ref, acc_ref, full_ref, far_a_ref, far_b_ref, left, part_a_ref, part_b_ref):
    h = far_a_ref.shape[1]
    for at, far in ((0, far_a_ref), (h, far_b_ref)):
        cols = pl.ds(at, h)
        left[:, cols] = (acc_ref[:, cols] + dot(amps_ref[...], far[...])).astype(BF)
    part = columns_for(2, pairs, place_ref, left, full_ref, far_a_ref, far_b_ref).astype(BF)
    part_a_ref[...] = part[:, :h]
    part_b_ref[...] = part[:, h:]


def second_kernel(pairs, place_ref, left, full_ref, far_a_ref, far_b_ref, *refs):
    h = far_a_ref.shape[1]
    for n, d in enumerate((1, 3, 0)):
        part = columns_for(d, pairs, place_ref, left, full_ref, far_a_ref, far_b_ref)
        for ref, half in zip(refs[2 * n : 2 * n + 2], (part[:, :h], part[:, h:])):
            ref[...] = half.astype(ref.dtype)


def columns_for(d, pairs, place_ref, left, full_ref, far_a_ref, far_b_ref):
    last = (place_ref[1] + NZ // 2) % NZ
    at = pl.ds(pl.multiple_of((place_ref[0] + d) % NY * pairs, 32), pairs)
    far = jnp.concatenate([far_a_ref[at], far_b_ref[at]], axis=1)
    block = jnp.concatenate([jnp.where(last == k, far, full_ref[k, at]) for k in range(NZ)], axis=0)
    return dot_t(left[...], block)


def out_kernel(pairs, first, place_ref, total_ref, amps_ref, own_ref, *refs):
    send_refs, (total, rows, amps, sems) = refs[:-4], refs[-4:]
    y = place_ref[0]
    width = total_ref.shape[1]
    step = amps.shape[2]
    copies = [
        pltpu.make_async_copy(amps_ref.at[:, pl.ds(k * step, step)], amps.at[k], sems.at[k])
        for k in range(amps.shape[0])
    ]
    for copy in copies:
        copy.start()
    for d in range(NY):
        block = total_ref[pl.ds(pl.multiple_of((y + d) % NY * pairs, 32), pairs)]
        total[d * pairs : (d + 1) * pairs] = block
        rows[d * pairs : (d + 1) * pairs] = block.astype(BF)
    for k, copy in enumerate(copies):
        n, part = divmod(first + k * step, width)
        cols = pl.ds(k * step, step)
        copy.wait()
        prod = dot(rows[...], amps[k])
        prod += jnp.where(y == n, total[:, part : part + step], 0.0)
        own_ref[:, cols] = prod[:pairs]
        for d in range(1, NY):
            send_refs[d - 1][:, cols] = prod[d * pairs : (d + 1) * pairs].astype(send_refs[d - 1].dtype)


def out_products(place, total, amps_i, first, pairs, kept):
    rows, cols = amps_i.shape
    types = [F32 if d in (0, kept) else BF for d in range(NY)]
    step = total.shape[1] // 2
    return pl.pallas_call(
        functools.partial(out_kernel, pairs, first),
        out_shape=[jax.ShapeDtypeStruct((pairs, cols), t) for t in types],
        in_specs=[SMEM, VMEM, ANY],
        out_specs=[VMEM] * NY,
        scratch_shapes=[
            pltpu.VMEM(total.shape, F32),
            pltpu.VMEM(total.shape, BF),
            pltpu.VMEM((cols // step, rows, step), BF),
            pltpu.SemaphoreType.DMA((cols // step,)),
        ],
        compiler_params=params(10),
        cost_estimate=cost(2 * total.size * cols),
    )(place, total, amps_i)


def collect(own, two, direct, kept, step):
    relay = (kept + shift(two, "y", step).astype(F32)).astype(BF)
    return own + shift(direct, "y", -step).astype(F32) + shift(relay, "y", step).astype(F32)


def shards(pair_table, cholesky, amplitudes, denominators):
    y, z, x, c = (lax.axis_index(a) for a in ("y", "z", "x", "c"))
    place = jnp.stack([y, z, c])
    amps = amplitudes[0]
    pairs, naux = amps.shape[0], cholesky.shape[1]
    aux = -(-naux // (128 * NY)) * 128
    width = NZ * pairs
    rows = NY * pairs
    third = pairs // NX

    early = 4 * NY * width // 8
    amps_i0 = lax.all_gather(amps[:, :early], "z", axis=0, tiled=True)
    by_z = jnp.transpose(amps.reshape(pairs, NY, NZ, pairs), (0, 2, 1, 3)).reshape(pairs, NY * width)

    own = jnp.pad(jnp.transpose(cholesky[0]), ((0, 0), (0, NY * aux - naux)))
    own = jnp.transpose(own.reshape(NX, third, NY, aux), (0, 2, 1, 3)).reshape(NX * NY, third, aux)
    held = lax.all_to_all(own, ("x", "y"), split_axis=0, concat_axis=0, tiled=True).reshape(NX, NY, third, aux)
    sent, by_z = choose(swap_kernel, (held, by_z), place, pair_table, held, by_z)
    (mine,) = choose(mine_kernel, (held,), place, pair_table, held, shift(sent, "c", 1))
    amps_j = lax.all_gather(by_z, "y", axis=0, tiled=True)
    parts = lax.all_to_all(mine, "x", split_axis=0, concat_axis=0, tiled=True)
    chosen = join(parts, amps_i0).reshape(rows, aux)

    dist, blocks = [0], [chosen]
    fore = back = chosen
    for s in range(1, NZ // 2):
        fore, back = shift(fore, "z", 1), shift(back, "z", -1)
        dist += [-s, s]
        blocks += [fore, back]
    far_a, far_b, later = last_step(fore, back, amps[:, early:])
    far_a, far_b = shift(far_a, "z", 1), shift(far_b, "z", -1)
    amps_i1 = lax.all_gather(later, "z", axis=0, tiled=True)

    n = len(blocks) - 2
    acc = add_left(place, amps_j, dist[:n], blocks[:n])
    acc, full, amps_last = add_left(place, amps_j, dist[n:], blocks[n:], acc)
    part, kept = (jax.ShapeDtypeStruct((rows, width // 2), t) for t in (BF, F32))
    left, two_a, two_b = pl.pallas_call(
        functools.partial(first_kernel, pairs),
        out_shape=[jax.ShapeDtypeStruct((rows, aux), BF), part, part],
        in_specs=[SMEM] + [VMEM] * 5,
        out_specs=[VMEM] * 3,
        compiler_params=params(8),
        cost_estimate=cost(2 * rows * aux * (rows + width)),
    )(place, amps_last, acc, full, far_a, far_b)
    one_a, one_b, three_a, three_b, own_a, own_b = pl.pallas_call(
        functools.partial(second_kernel, pairs),
        out_shape=[kept, part, part, kept, kept, kept],
        in_specs=[SMEM] + [VMEM] * 4,
        out_specs=[VMEM] * 6,
        compiler_params=params(8),
        cost_estimate=cost(6 * rows * aux * width),
    )(place, left, full, far_a, far_b)
    total = [collect(own_a, two_a, three_a, one_a, 1), collect(own_b, two_b, one_b, three_b, -1)]
    total = jnp.concatenate(total, axis=1)

    own, one, two, three = out_products(place, total, amps_i0, 0, pairs, 1)
    outs = [collect(own, two, three, one, 1)]
    own, one, two, three = out_products(place, total, amps_i1, early, pairs, 3)
    outs.append(collect(own, two, one, three, -1))
    return (-jnp.concatenate(outs, axis=1) / denominators[0]).astype(BF)[None]


def solution(mesh):
    grid = Mesh(mesh.devices.reshape(NY, NZ, NX, NC), ("y", "z", "x", "c"))
    ka, row = ("x", "c"), ("y", "z")
    in_specs = (P(), P(ka, None, row), P(ka, row, None), P(ka, row, None))
    return jax.shard_map(shards, mesh=grid, in_specs=in_specs, out_specs=P(ka, row, None), check_vma=False)
```

```python
import functools

import jax
import jax.numpy as jnp
from jax import lax
from jax.experimental import pallas as pl
from jax.experimental.pallas import tpu as pltpu
from jax.sharding import Mesh
from jax.sharding import PartitionSpec as P

NY, NZ, NX, NC = 4, 8, 4, 2
BF, F32 = jnp.bfloat16, jnp.float32
SIZES = {"y": NY, "z": NZ, "x": NX, "c": NC}
ANY = pl.BlockSpec(memory_space=pl.ANY)
VMEM = pl.BlockSpec(memory_space=pltpu.VMEM)
SMEM = pl.BlockSpec(memory_space=pltpu.SMEM)


def params(mib):
    return pltpu.CompilerParams(vmem_limit_bytes=mib * 2**20)


def shift(block, axis, step):
    n = SIZES[axis]
    with jax.named_scope(f"{axis}{step}_{block.size * 2 // 1000}kB"):
        return lax.ppermute(block, axis, [(i, (i + step) % n) for i in range(n)])


def dot(a, b):
    return jnp.dot(a, b, preferred_element_type=F32)


def dot_t(a, b):
    return lax.dot_general(a, b, (((1,), (1,)), ((), ())), preferred_element_type=F32)


def cost(flops):
    return pl.CostEstimate(flops=flops, bytes_accessed=8 * 2**20, transcendentals=0)


def swap_kernel(place_ref, table_ref, held_ref, amps_ref, sent_ref, out_ref, sems):
    c = place_ref[2]
    copies = [pltpu.make_async_copy(amps_ref, out_ref, sems.at[NX])]
    copies[0].start()
    for k in range(NX):
        want = table_ref[k * NC + 1 - c]
        copies.append(pltpu.make_async_copy(held_ref.at[want >> 1], sent_ref.at[k], sems.at[k]))
        copies[-1].start()
    for copy in copies:
        copy.wait()


def mine_kernel(place_ref, table_ref, held_ref, sent_ref, mine_ref, sems):
    c = place_ref[2]
    for k in range(NX):
        want = table_ref[k * NC + c]
        here = (want & 1) == c

        @pl.when(here)
        def _():
            pltpu.make_async_copy(held_ref.at[want >> 1], mine_ref.at[k], sems.at[k]).start()

        @pl.when(jnp.logical_not(here))
        def _():
            pltpu.make_async_copy(sent_ref.at[k], mine_ref.at[k], sems.at[k]).start()

    for k in range(NX):
        pltpu.make_async_copy(sent_ref.at[k], mine_ref.at[k], sems.at[k]).wait()


def choose(kernel, results, place, table, *arrays):
    return pl.pallas_call(
        kernel,
        out_shape=[jax.ShapeDtypeStruct(a.shape, a.dtype) for a in results],
        in_specs=[SMEM, SMEM] + [ANY] * len(arrays),
        out_specs=[ANY] * len(results),
        scratch_shapes=[pltpu.SemaphoreType.DMA((NX + 1,))],
        compiler_params=params(2),
    )(place, table, *arrays)


def join_kernel(parts_ref, chosen_ref, sems):
    copies = [pltpu.make_async_copy(parts_ref.at[k], chosen_ref.at[:, k], sems.at[k]) for k in range(NX)]
    for copy in copies:
        copy.start()
    for copy in copies:
        copy.wait()


def join(parts):
    nx, ny, third, aux = parts.shape
    return pl.pallas_call(
        join_kernel,
        out_shape=jax.ShapeDtypeStruct((ny, nx, third, aux), BF),
        in_specs=[ANY],
        out_specs=ANY,
        scratch_shapes=[pltpu.SemaphoreType.DMA((NX,))],
        compiler_params=params(2),
    )(parts)


def same_kernel(block_ref, other_ref, same_ref):
    pass


def after(block, other):
    return pl.pallas_call(
        same_kernel,
        out_shape=jax.ShapeDtypeStruct(block.shape, BF),
        in_specs=[ANY] * 2,
        out_specs=ANY,
        input_output_aliases={0: 0},
        compiler_params=params(62),
    )(block, other)


def last_kernel(fore_ref, back_ref, late_ref, a_ref, b_ref, later_ref, sems):
    h = a_ref.shape[1]
    copies = [
        pltpu.make_async_copy(fore_ref.at[:, pl.ds(0, h)], a_ref, sems.at[0]),
        pltpu.make_async_copy(back_ref.at[:, pl.ds(h, h)], b_ref, sems.at[1]),
        pltpu.make_async_copy(late_ref, later_ref, sems.at[2]),
    ]
    for copy in copies:
        copy.start()
    for copy in copies:
        copy.wait()


def last_step(fore, back, late):
    rows, aux = fore.shape
    half = jax.ShapeDtypeStruct((rows, aux // 2), BF)
    return pl.pallas_call(
        last_kernel,
        out_shape=[half, half, jax.ShapeDtypeStruct(late.shape, BF)],
        in_specs=[ANY] * 3,
        out_specs=[ANY] * 3,
        scratch_shapes=[pltpu.SemaphoreType.DMA((3,))],
        compiler_params=params(2),
    )(fore, back, late)


def left_kernel(dist, place_ref, amps_ref, *refs):
    blocks, (left_ref, full_ref, last_ref) = refs[:-3], refs[-3:]
    z, rows = place_ref[1], blocks[0].shape[0]

    def amps(d):
        return amps_ref[:, pl.ds(pl.multiple_of((z + NZ + d) % NZ * rows, 128), rows)]

    for n, d in enumerate(dist):
        block = blocks[n][...]
        full_ref[(z + NZ + d) % NZ] = block
        part = dot(amps(d), block)
        if n:
            left_ref[...] += part
        else:
            left_ref[...] = block.astype(F32) + part
    last_ref[...] = amps(NZ // 2)


def add_left(place, amps, dist, blocks):
    rows, aux = blocks[0].shape
    n = len(dist)
    shapes = [((rows, aux), F32), ((NZ, rows, aux), BF), ((rows, rows), BF)]
    return pl.pallas_call(
        functools.partial(left_kernel, dist),
        out_shape=[jax.ShapeDtypeStruct(*a) for a in shapes],
        in_specs=[SMEM, VMEM] + [VMEM] * n,
        out_specs=[VMEM] * len(shapes),
        compiler_params=params(8),
        cost_estimate=cost(2 * rows * aux * rows * n),
    )(place, amps, *blocks)


def first_kernel(pairs, place_ref, amps_ref, acc_ref, full_ref, far_a_ref, far_b_ref, left, part_a_ref, part_b_ref):
    h = far_a_ref.shape[1]
    for at, far in ((0, far_a_ref), (h, far_b_ref)):
        cols = pl.ds(at, h)
        left[:, cols] = (acc_ref[:, cols] + dot(amps_ref[...], far[...])).astype(BF)
    part = columns_for(2, pairs, place_ref, left, full_ref, far_a_ref, far_b_ref).astype(BF)
    part_a_ref[...] = part[:, :h]
    part_b_ref[...] = part[:, h:]


def second_kernel(pairs, place_ref, left, full_ref, far_a_ref, far_b_ref, amps_ref, *refs):
    copy_ref, sem = refs[-2:]
    copy = pltpu.make_async_copy(amps_ref, copy_ref, sem)
    copy.start()
    h = far_a_ref.shape[1]
    for n, d in enumerate((1, 3, 0)):
        part = columns_for(d, pairs, place_ref, left, full_ref, far_a_ref, far_b_ref)
        for ref, half in zip(refs[2 * n : 2 * n + 2], (part[:, :h], part[:, h:])):
            ref[...] = half.astype(ref.dtype)
    copy.wait()


def columns_for(d, pairs, place_ref, left, full_ref, far_a_ref, far_b_ref):
    last = (place_ref[1] + NZ // 2) % NZ
    at = pl.ds(pl.multiple_of((place_ref[0] + d) % NY * pairs, 32), pairs)
    far = jnp.concatenate([far_a_ref[at], far_b_ref[at]], axis=1)
    block = jnp.concatenate([jnp.where(last == k, far, full_ref[k, at]) for k in range(NZ)], axis=0)
    return dot_t(left[...], block)


def out_kernel(pairs, first, place_ref, total_ref, amps_ref, own_ref, *refs):
    send_refs, (total, rows) = refs[:-2], refs[-2:]
    y = place_ref[0]
    width = total_ref.shape[1]
    step = width // 2
    for d in range(NY):
        block = total_ref[pl.ds(pl.multiple_of((y + d) % NY * pairs, 32), pairs)]
        total[d * pairs : (d + 1) * pairs] = block
        rows[d * pairs : (d + 1) * pairs] = block.astype(BF)
    for k in range(amps_ref.shape[1] // step):
        n, part = divmod(first + k * step, width)
        cols = pl.ds(k * step, step)
        prod = dot(rows[...], amps_ref[:, cols])
        prod += jnp.where(y == n, total[:, part : part + step], 0.0)
        own_ref[:, cols] = prod[:pairs]
        for d in range(1, NY):
            send_refs[d - 1][:, cols] = prod[d * pairs : (d + 1) * pairs].astype(send_refs[d - 1].dtype)


def out_products(place, total, amps_i, first, pairs, kept):
    rows, cols = amps_i.shape
    types = [F32 if d in (0, kept) else BF for d in range(NY)]
    return pl.pallas_call(
        functools.partial(out_kernel, pairs, first),
        out_shape=[jax.ShapeDtypeStruct((pairs, cols), t) for t in types],
        in_specs=[SMEM, VMEM, VMEM],
        out_specs=[VMEM] * NY,
        scratch_shapes=[
            pltpu.VMEM(total.shape, F32),
            pltpu.VMEM(total.shape, BF),
        ],
        compiler_params=params(10),
        cost_estimate=cost(2 * total.size * cols),
    )(place, total, amps_i)


def collect(own, two, direct, kept, step):
    relay = (kept + shift(two, "y", step).astype(F32)).astype(BF)
    return own + shift(direct, "y", -step).astype(F32) + shift(relay, "y", step).astype(F32)


def shards(pair_table, cholesky, amplitudes, denominators):
    y, z, x, c = (lax.axis_index(a) for a in ("y", "z", "x", "c"))
    place = jnp.stack([y, z, c])
    amps = amplitudes[0]
    pairs, naux = amps.shape[0], cholesky.shape[1]
    aux = -(-naux // (128 * NY)) * 128
    width = NZ * pairs
    rows = NY * pairs
    third = pairs // NX

    early = 4 * NY * width // 8
    amps_i0 = lax.all_gather(amps[:, :early], "z", axis=0, tiled=True)
    by_z = jnp.transpose(amps.reshape(pairs, NY, NZ, pairs), (0, 2, 1, 3)).reshape(pairs, NY * width)

    own = jnp.pad(jnp.transpose(cholesky[0]), ((0, 0), (0, NY * aux - naux)))
    own = jnp.transpose(own.reshape(NX, third, NY, aux), (0, 2, 1, 3)).reshape(NX * NY, third, aux)
    held = lax.all_to_all(own, ("x", "y"), split_axis=0, concat_axis=0, tiled=True).reshape(NX, NY, third, aux)
    sent, by_z = choose(swap_kernel, (held, by_z), place, pair_table, held, by_z)
    (mine,) = choose(mine_kernel, (held,), place, pair_table, held, shift(sent, "c", 1))
    amps_j = lax.all_gather(by_z, "y", axis=0, tiled=True)
    parts = lax.all_to_all(mine, "x", split_axis=0, concat_axis=0, tiled=True)
    chosen = after(join(parts).reshape(rows, aux), amps_i0)

    dist, blocks = [0], [chosen]
    fore = back = chosen
    for s in range(1, NZ // 2):
        fore, back = shift(fore, "z", 1), shift(back, "z", -1)
        dist += [-s, s]
        blocks += [fore, back]
    far_a, far_b, later = last_step(fore, back, amps[:, early:])
    far_a, far_b = shift(far_a, "z", 1), shift(far_b, "z", -1)
    amps_i1 = lax.all_gather(later, "z", axis=0, tiled=True)

    acc, full, amps_last = add_left(place, amps_j, dist, blocks)
    part, kept = (jax.ShapeDtypeStruct((rows, width // 2), t) for t in (BF, F32))
    left, two_a, two_b = pl.pallas_call(
        functools.partial(first_kernel, pairs),
        out_shape=[jax.ShapeDtypeStruct((rows, aux), BF), part, part],
        in_specs=[SMEM] + [VMEM] * 5,
        out_specs=[VMEM] * 3,
        compiler_params=params(8),
        cost_estimate=cost(2 * rows * aux * (rows + width)),
    )(place, amps_last, acc, full, far_a, far_b)
    one_a, one_b, three_a, three_b, own_a, own_b, amps_i0 = pl.pallas_call(
        functools.partial(second_kernel, pairs),
        out_shape=[kept, part, part, kept, kept, kept, jax.ShapeDtypeStruct(amps_i0.shape, BF)],
        in_specs=[SMEM] + [VMEM] * 4 + [ANY],
        out_specs=[VMEM] * 7,
        scratch_shapes=[pltpu.SemaphoreType.DMA],
        compiler_params=params(8),
        cost_estimate=cost(6 * rows * aux * width),
    )(place, left, full, far_a, far_b, amps_i0)
    total = [collect(own_a, two_a, three_a, one_a, 1), collect(own_b, two_b, one_b, three_b, -1)]
    total = jnp.concatenate(total, axis=1)

    own, one, two, three = out_products(place, total, amps_i0, 0, pairs, 1)
    outs = [collect(own, two, three, one, 1)]
    own, one, two, three = out_products(place, total, amps_i1, early, pairs, 3)
    outs.append(collect(own, two, one, three, -1))
    return (-jnp.concatenate(outs, axis=1) / denominators[0]).astype(BF)[None]


def solution(mesh):
    grid = Mesh(mesh.devices.reshape(NY, NZ, NX, NC), ("y", "z", "x", "c"))
    ka, row = ("x", "c"), ("y", "z")
    in_specs = (P(), P(ka, None, row), P(ka, row, None), P(ka, row, None))
    return jax.shard_map(shards, mesh=grid, in_specs=in_specs, out_specs=P(ka, row, None), check_vma=False)
```

```python
import functools

import jax
import jax.numpy as jnp
from jax import lax
from jax.experimental import pallas as pl
from jax.experimental.pallas import tpu as pltpu
from jax.sharding import Mesh
from jax.sharding import PartitionSpec as P

NY, NZ, NX, NC = 4, 8, 4, 2
BF, F32 = jnp.bfloat16, jnp.float32
SIZES = {"y": NY, "z": NZ, "x": NX, "c": NC}
ANY = pl.BlockSpec(memory_space=pl.ANY)
VMEM = pl.BlockSpec(memory_space=pltpu.VMEM)
SMEM = pl.BlockSpec(memory_space=pltpu.SMEM)


def params(mib):
    return pltpu.CompilerParams(vmem_limit_bytes=mib * 2**20)


def shift(block, axis, step):
    n = SIZES[axis]
    with jax.named_scope(f"{axis}{step}_{block.size * 2 // 1000}kB"):
        return lax.ppermute(block, axis, [(i, (i + step) % n) for i in range(n)])


def dot(a, b):
    return jnp.dot(a, b, preferred_element_type=F32)


def dot_t(a, b):
    return lax.dot_general(a, b, (((1,), (1,)), ((), ())), preferred_element_type=F32)


def cost(flops):
    return pl.CostEstimate(flops=flops, bytes_accessed=8 * 2**20, transcendentals=0)


def swap_kernel(place_ref, table_ref, held_ref, amps_ref, sent_ref, out_ref, sems):
    c = place_ref[2]
    copies = [pltpu.make_async_copy(amps_ref, out_ref, sems.at[NX])]
    copies[0].start()
    for k in range(NX):
        want = table_ref[k * NC + 1 - c]
        copies.append(pltpu.make_async_copy(held_ref.at[want >> 1], sent_ref.at[k], sems.at[k]))
        copies[-1].start()
    for copy in copies:
        copy.wait()


def mine_kernel(place_ref, table_ref, held_ref, sent_ref, amps_ref, mine_ref, out_ref, sems):
    c = place_ref[2]
    amps = pltpu.make_async_copy(amps_ref, out_ref, sems.at[NX])
    amps.start()
    for k in range(NX):
        want = table_ref[k * NC + c]
        here = (want & 1) == c

        @pl.when(here)
        def _():
            pltpu.make_async_copy(held_ref.at[want >> 1], mine_ref.at[k], sems.at[k]).start()

        @pl.when(jnp.logical_not(here))
        def _():
            pltpu.make_async_copy(sent_ref.at[k], mine_ref.at[k], sems.at[k]).start()

    for k in range(NX):
        pltpu.make_async_copy(sent_ref.at[k], mine_ref.at[k], sems.at[k]).wait()
    amps.wait()


def choose(kernel, results, place, table, *arrays):
    return pl.pallas_call(
        kernel,
        out_shape=[jax.ShapeDtypeStruct(a.shape, a.dtype) for a in results],
        in_specs=[SMEM, SMEM] + [ANY] * len(arrays),
        out_specs=[ANY] * len(results),
        scratch_shapes=[pltpu.SemaphoreType.DMA((NX + 1,))],
        compiler_params=params(2),
    )(place, table, *arrays)


def join_kernel(parts_ref, chosen_ref, sems):
    copies = [pltpu.make_async_copy(parts_ref.at[k], chosen_ref.at[:, k], sems.at[k]) for k in range(NX)]
    for copy in copies:
        copy.start()
    for copy in copies:
        copy.wait()


def join(parts):
    nx, ny, third, aux = parts.shape
    return pl.pallas_call(
        join_kernel,
        out_shape=jax.ShapeDtypeStruct((ny, nx, third, aux), BF),
        in_specs=[ANY],
        out_specs=ANY,
        scratch_shapes=[pltpu.SemaphoreType.DMA((NX,))],
        compiler_params=params(2),
    )(parts)


def same_kernel(block_ref, other_ref, same_ref):
    pass


def after(block, other):
    return pl.pallas_call(
        same_kernel,
        out_shape=jax.ShapeDtypeStruct(block.shape, BF),
        in_specs=[ANY] * 2,
        out_specs=ANY,
        input_output_aliases={0: 0},
        compiler_params=params(62),
    )(block, other)


def last_kernel(fore_ref, back_ref, a_ref, b_ref, sems):
    h = a_ref.shape[1]
    copies = [
        pltpu.make_async_copy(fore_ref.at[:, pl.ds(0, h)], a_ref, sems.at[0]),
        pltpu.make_async_copy(back_ref.at[:, pl.ds(h, h)], b_ref, sems.at[1]),
    ]
    for copy in copies:
        copy.start()
    for copy in copies:
        copy.wait()


def last_step(fore, back):
    rows, aux = fore.shape
    half = jax.ShapeDtypeStruct((rows, aux // 2), BF)
    return pl.pallas_call(
        last_kernel,
        out_shape=[half, half],
        in_specs=[ANY] * 2,
        out_specs=[ANY] * 2,
        scratch_shapes=[pltpu.SemaphoreType.DMA((2,))],
        compiler_params=params(2),
    )(fore, back)


def left_kernel(dist, place_ref, amps_ref, *refs):
    blocks, (left_ref, full_ref, last_ref) = refs[:-3], refs[-3:]
    z, rows = place_ref[1], blocks[0].shape[0]

    def amps(d):
        return amps_ref[:, pl.ds(pl.multiple_of((z + NZ + d) % NZ * rows, 128), rows)]

    for n, d in enumerate(dist):
        block = blocks[n][...]
        full_ref[(z + NZ + d) % NZ] = block
        part = dot(amps(d), block)
        if n:
            left_ref[...] += part
        else:
            left_ref[...] = block.astype(F32) + part
    last_ref[...] = amps(NZ // 2)


def add_left(place, amps, dist, blocks):
    rows, aux = blocks[0].shape
    n = len(dist)
    shapes = [((rows, aux), F32), ((NZ, rows, aux), BF), ((rows, rows), BF)]
    return pl.pallas_call(
        functools.partial(left_kernel, dist),
        out_shape=[jax.ShapeDtypeStruct(*a) for a in shapes],
        in_specs=[SMEM, VMEM] + [VMEM] * n,
        out_specs=[VMEM] * len(shapes),
        compiler_params=params(8),
        cost_estimate=cost(2 * rows * aux * rows * n),
    )(place, amps, *blocks)


def first_kernel(pairs, place_ref, amps_ref, acc_ref, full_ref, far_a_ref, far_b_ref, left, part_a_ref, part_b_ref):
    h = far_a_ref.shape[1]
    for at, far in ((0, far_a_ref), (h, far_b_ref)):
        cols = pl.ds(at, h)
        left[:, cols] = (acc_ref[:, cols] + dot(amps_ref[...], far[...])).astype(BF)
    part = columns_for(2, pairs, place_ref, left, full_ref, far_a_ref, far_b_ref).astype(BF)
    part_a_ref[...] = part[:, :h]
    part_b_ref[...] = part[:, h:]


def second_kernel(pairs, place_ref, left, full_ref, far_a_ref, far_b_ref, amps_ref, *refs):
    copy_ref, sem = refs[-2:]
    copy = pltpu.make_async_copy(amps_ref, copy_ref, sem)
    copy.start()
    h = far_a_ref.shape[1]
    for n, d in enumerate((1, 3, 0)):
        part = columns_for(d, pairs, place_ref, left, full_ref, far_a_ref, far_b_ref)
        for ref, half in zip(refs[2 * n : 2 * n + 2], (part[:, :h], part[:, h:])):
            ref[...] = half.astype(ref.dtype)
    copy.wait()


def columns_for(d, pairs, place_ref, left, full_ref, far_a_ref, far_b_ref):
    last = (place_ref[1] + NZ // 2) % NZ
    at = pl.ds(pl.multiple_of((place_ref[0] + d) % NY * pairs, 32), pairs)
    far = jnp.concatenate([far_a_ref[at], far_b_ref[at]], axis=1)
    block = jnp.concatenate([jnp.where(last == k, far, full_ref[k, at]) for k in range(NZ)], axis=0)
    return dot_t(left[...], block)


def out_kernel(pairs, first, place_ref, total_ref, amps_ref, own_ref, *refs):
    send_refs, (total, rows) = refs[:-2], refs[-2:]
    y = place_ref[0]
    width = total_ref.shape[1]
    step = width // 2
    for d in range(NY):
        block = total_ref[pl.ds(pl.multiple_of((y + d) % NY * pairs, 32), pairs)]
        total[d * pairs : (d + 1) * pairs] = block
        rows[d * pairs : (d + 1) * pairs] = block.astype(BF)
    for k in range(amps_ref.shape[1] // step):
        n, part = divmod(first + k * step, width)
        cols = pl.ds(k * step, step)
        prod = dot(rows[...], amps_ref[:, cols])
        prod += jnp.where(y == n, total[:, part : part + step], 0.0)
        own_ref[:, cols] = prod[:pairs]
        for d in range(1, NY):
            send_refs[d - 1][:, cols] = prod[d * pairs : (d + 1) * pairs].astype(send_refs[d - 1].dtype)


def out_products(place, total, amps_i, first, pairs, kept):
    rows, cols = amps_i.shape
    types = [F32 if d in (0, kept) else BF for d in range(NY)]
    return pl.pallas_call(
        functools.partial(out_kernel, pairs, first),
        out_shape=[jax.ShapeDtypeStruct((pairs, cols), t) for t in types],
        in_specs=[SMEM, VMEM, VMEM],
        out_specs=[VMEM] * NY,
        scratch_shapes=[
            pltpu.VMEM(total.shape, F32),
            pltpu.VMEM(total.shape, BF),
        ],
        compiler_params=params(10),
        cost_estimate=cost(2 * total.size * cols),
    )(place, total, amps_i)


def collect(own, two, direct, kept, step):
    relay = (kept + shift(two, "y", step).astype(F32)).astype(BF)
    return own + shift(direct, "y", -step).astype(F32) + shift(relay, "y", step).astype(F32)


def shards(pair_table, cholesky, amplitudes, denominators):
    y, z, x, c = (lax.axis_index(a) for a in ("y", "z", "x", "c"))
    place = jnp.stack([y, z, c])
    amps = amplitudes[0]
    pairs, naux = amps.shape[0], cholesky.shape[1]
    aux = -(-naux // (128 * NY)) * 128
    width = NZ * pairs
    rows = NY * pairs
    third = pairs // NX

    early = 4 * NY * width // 8
    amps_i0 = lax.all_gather(amps[:, :early], "z", axis=0, tiled=True)
    by_z = jnp.transpose(amps.reshape(pairs, NY, NZ, pairs), (0, 2, 1, 3)).reshape(pairs, NY * width)

    own = jnp.pad(jnp.transpose(cholesky[0]), ((0, 0), (0, NY * aux - naux)))
    own = jnp.transpose(own.reshape(NX, third, NY, aux), (0, 2, 1, 3)).reshape(NX * NY, third, aux)
    held = lax.all_to_all(own, ("x", "y"), split_axis=0, concat_axis=0, tiled=True).reshape(NX, NY, third, aux)
    sent, by_z = choose(swap_kernel, (held, by_z), place, pair_table, held, by_z)
    late = amps[:, early:]
    mine, later = choose(mine_kernel, (held, late), place, pair_table, held, shift(sent, "c", 1), late)
    amps_j = lax.all_gather(by_z, "y", axis=0, tiled=True)
    parts = lax.all_to_all(mine, "x", split_axis=0, concat_axis=0, tiled=True)
    chosen = after(join(parts).reshape(rows, aux), amps_i0)

    dist, blocks = [0], [chosen]
    fore = back = chosen
    for s in range(1, NZ // 2):
        fore, back = shift(fore, "z", 1), shift(back, "z", -1)
        dist += [-s, s]
        blocks += [fore, back]
    far_a, far_b = last_step(fore, back)
    far_a, far_b = shift(far_a, "z", 1), shift(far_b, "z", -1)
    amps_i1 = lax.all_gather(later, "z", axis=0, tiled=True)

    acc, full, amps_last = add_left(place, amps_j, dist, blocks)
    part, kept = (jax.ShapeDtypeStruct((rows, width // 2), t) for t in (BF, F32))
    left, two_a, two_b = pl.pallas_call(
        functools.partial(first_kernel, pairs),
        out_shape=[jax.ShapeDtypeStruct((rows, aux), BF), part, part],
        in_specs=[SMEM] + [VMEM] * 5,
        out_specs=[VMEM] * 3,
        compiler_params=params(8),
        cost_estimate=cost(2 * rows * aux * (rows + width)),
    )(place, amps_last, acc, full, far_a, far_b)
    one_a, one_b, three_a, three_b, own_a, own_b, amps_i0 = pl.pallas_call(
        functools.partial(second_kernel, pairs),
        out_shape=[kept, part, part, kept, kept, kept, jax.ShapeDtypeStruct(amps_i0.shape, BF)],
        in_specs=[SMEM] + [VMEM] * 4 + [ANY],
        out_specs=[VMEM] * 7,
        scratch_shapes=[pltpu.SemaphoreType.DMA],
        compiler_params=params(8),
        cost_estimate=cost(6 * rows * aux * width),
    )(place, left, full, far_a, far_b, amps_i0)
    relay_a, relay_b = shift(two_a, "y", 1), shift(two_b, "y", -1)
    direct_a, direct_b = shift(three_a, "y", -1), shift(one_b, "y", 1)
    direct = jnp.concatenate([direct_a, direct_b], axis=1).astype(F32)
    relay_a = shift((one_a + relay_a.astype(F32)).astype(BF), "y", 1)
    relay_b = shift((three_b + relay_b.astype(F32)).astype(BF), "y", -1)
    own = jnp.concatenate([own_a, own_b], axis=1)
    total = own + direct + jnp.concatenate([relay_a, relay_b], axis=1).astype(F32)

    own, one, two, three = out_products(place, total, amps_i0, 0, pairs, 1)
    outs = [collect(own, two, three, one, 1)]
    own, one, two, three = out_products(place, total, amps_i1, early, pairs, 3)
    outs.append(collect(own, two, one, three, -1))
    return (-jnp.concatenate(outs, axis=1) / denominators[0]).astype(BF)[None]


def solution(mesh):
    grid = Mesh(mesh.devices.reshape(NY, NZ, NX, NC), ("y", "z", "x", "c"))
    ka, row = ("x", "c"), ("y", "z")
    in_specs = (P(), P(ka, None, row), P(ka, row, None), P(ka, row, None))
    return jax.shard_map(shards, mesh=grid, in_specs=in_specs, out_specs=P(ka, row, None), check_vma=False)
```

```python
import functools

import jax
import jax.numpy as jnp
from jax import lax
from jax.experimental import pallas as pl
from jax.experimental.pallas import tpu as pltpu
from jax.sharding import Mesh
from jax.sharding import PartitionSpec as P

NY, NZ, NX, NC = 4, 8, 4, 2
BF, F32 = jnp.bfloat16, jnp.float32
SIZES = {"y": NY, "z": NZ, "x": NX, "c": NC}
ANY = pl.BlockSpec(memory_space=pl.ANY)
VMEM = pl.BlockSpec(memory_space=pltpu.VMEM)
SMEM = pl.BlockSpec(memory_space=pltpu.SMEM)


def params(mib):
    return pltpu.CompilerParams(vmem_limit_bytes=mib * 2**20)


def shift(block, axis, step):
    n = SIZES[axis]
    with jax.named_scope(f"{axis}{step}_{block.size * 2 // 1000}kB"):
        return lax.ppermute(block, axis, [(i, (i + step) % n) for i in range(n)])


def dot(a, b):
    return jnp.dot(a, b, preferred_element_type=F32)


def dot_t(a, b):
    return lax.dot_general(a, b, (((1,), (1,)), ((), ())), preferred_element_type=F32)


def cost(flops):
    return pl.CostEstimate(flops=flops, bytes_accessed=8 * 2**20, transcendentals=0)


def swap_kernel(place_ref, table_ref, held_ref, amps_ref, sent_ref, out_ref, sems):
    c = place_ref[2]
    copies = [pltpu.make_async_copy(amps_ref, out_ref, sems.at[NX])]
    copies[0].start()
    for k in range(NX):
        want = table_ref[k * NC + 1 - c]
        copies.append(pltpu.make_async_copy(held_ref.at[want >> 1], sent_ref.at[k], sems.at[k]))
        copies[-1].start()
    for copy in copies:
        copy.wait()


def mine_kernel(place_ref, table_ref, held_ref, sent_ref, amps_ref, mine_ref, out_ref, sems):
    c = place_ref[2]
    amps = pltpu.make_async_copy(amps_ref, out_ref, sems.at[NX])
    amps.start()
    for k in range(NX):
        want = table_ref[k * NC + c]
        here = (want & 1) == c

        @pl.when(here)
        def _():
            pltpu.make_async_copy(held_ref.at[want >> 1], mine_ref.at[k], sems.at[k]).start()

        @pl.when(jnp.logical_not(here))
        def _():
            pltpu.make_async_copy(sent_ref.at[k], mine_ref.at[k], sems.at[k]).start()

    for k in range(NX):
        pltpu.make_async_copy(sent_ref.at[k], mine_ref.at[k], sems.at[k]).wait()
    amps.wait()


def choose(kernel, results, place, table, *arrays):
    return pl.pallas_call(
        kernel,
        out_shape=[jax.ShapeDtypeStruct(a.shape, a.dtype) for a in results],
        in_specs=[SMEM, SMEM] + [ANY] * len(arrays),
        out_specs=[ANY] * len(results),
        scratch_shapes=[pltpu.SemaphoreType.DMA((NX + 1,))],
        compiler_params=params(2),
    )(place, table, *arrays)


def join_kernel(parts_ref, chosen_ref, sems):
    copies = [pltpu.make_async_copy(parts_ref.at[k], chosen_ref.at[:, k], sems.at[k]) for k in range(NX)]
    for copy in copies:
        copy.start()
    for copy in copies:
        copy.wait()


def join(parts):
    nx, ny, third, aux = parts.shape
    return pl.pallas_call(
        join_kernel,
        out_shape=jax.ShapeDtypeStruct((ny, nx, third, aux), BF),
        in_specs=[ANY],
        out_specs=ANY,
        scratch_shapes=[pltpu.SemaphoreType.DMA((NX,))],
        compiler_params=params(2),
    )(parts)


def same_kernel(block_ref, other_ref, same_ref):
    pass


def after(block, other):
    return pl.pallas_call(
        same_kernel,
        out_shape=jax.ShapeDtypeStruct(block.shape, BF),
        in_specs=[ANY] * 2,
        out_specs=ANY,
        input_output_aliases={0: 0},
        compiler_params=params(62),
    )(block, other)


def last_kernel(fore_ref, back_ref, a_ref, b_ref, sems):
    h = a_ref.shape[1]
    copies = [
        pltpu.make_async_copy(fore_ref.at[:, pl.ds(0, h)], a_ref, sems.at[0]),
        pltpu.make_async_copy(back_ref.at[:, pl.ds(h, h)], b_ref, sems.at[1]),
    ]
    for copy in copies:
        copy.start()
    for copy in copies:
        copy.wait()


def last_step(fore, back):
    rows, aux = fore.shape
    half = jax.ShapeDtypeStruct((rows, aux // 2), BF)
    return pl.pallas_call(
        last_kernel,
        out_shape=[half, half],
        in_specs=[ANY] * 2,
        out_specs=[ANY] * 2,
        scratch_shapes=[pltpu.SemaphoreType.DMA((2,))],
        compiler_params=params(2),
    )(fore, back)


def left_kernel(dist, place_ref, amps_ref, *refs):
    blocks, (left_ref, full_ref, last_ref) = refs[:-3], refs[-3:]
    z, rows = place_ref[1], blocks[0].shape[0]

    def amps(d):
        return amps_ref[:, pl.ds(pl.multiple_of((z + NZ + d) % NZ * rows, 128), rows)]

    for n, d in enumerate(dist):
        block = blocks[n][...]
        full_ref[(z + NZ + d) % NZ] = block
        part = dot(amps(d), block)
        if n:
            left_ref[...] += part
        else:
            left_ref[...] = block.astype(F32) + part
    last_ref[...] = amps(NZ // 2)


def add_left(place, amps, dist, blocks):
    rows, aux = blocks[0].shape
    n = len(dist)
    shapes = [((rows, aux), F32), ((NZ, rows, aux), BF), ((rows, rows), BF)]
    return pl.pallas_call(
        functools.partial(left_kernel, dist),
        out_shape=[jax.ShapeDtypeStruct(*a) for a in shapes],
        in_specs=[SMEM, VMEM] + [VMEM] * n,
        out_specs=[VMEM] * len(shapes),
        compiler_params=params(8),
        cost_estimate=cost(2 * rows * aux * rows * n),
    )(place, amps, *blocks)


def first_kernel(pairs, place_ref, amps_ref, acc_ref, full_ref, far_a_ref, far_b_ref, left, part_a_ref, part_b_ref):
    h = far_a_ref.shape[1]
    for at, far in ((0, far_a_ref), (h, far_b_ref)):
        cols = pl.ds(at, h)
        left[:, cols] = (acc_ref[:, cols] + dot(amps_ref[...], far[...])).astype(BF)
    part = columns_for(2, pairs, place_ref, left, full_ref, far_a_ref, far_b_ref).astype(BF)
    part_a_ref[...] = part[:, :h]
    part_b_ref[...] = part[:, h:]


def second_kernel(pairs, place_ref, left, full_ref, far_a_ref, far_b_ref, amps_ref, *refs):
    copy_ref, sem = refs[-2:]
    copy = pltpu.make_async_copy(amps_ref, copy_ref, sem)
    copy.start()
    h = far_a_ref.shape[1]
    for n, d in enumerate((1, 3, 0)):
        part = columns_for(d, pairs, place_ref, left, full_ref, far_a_ref, far_b_ref)
        for ref, half in zip(refs[2 * n : 2 * n + 2], (part[:, :h], part[:, h:])):
            ref[...] = half.astype(ref.dtype)
    copy.wait()


def columns_for(d, pairs, place_ref, left, full_ref, far_a_ref, far_b_ref):
    last = (place_ref[1] + NZ // 2) % NZ
    at = pl.ds(pl.multiple_of((place_ref[0] + d) % NY * pairs, 32), pairs)
    far = jnp.concatenate([far_a_ref[at], far_b_ref[at]], axis=1)
    block = jnp.concatenate([jnp.where(last == k, far, full_ref[k, at]) for k in range(NZ)], axis=0)
    return dot_t(left[...], block)


def out_kernel(pairs, first, place_ref, total_ref, amps_ref, own_ref, *refs):
    send_refs, (total, rows) = refs[:-2], refs[-2:]
    y = place_ref[0]
    width = total_ref.shape[1]
    step = width // 2
    for d in range(NY):
        block = total_ref[pl.ds(pl.multiple_of((y + d) % NY * pairs, 32), pairs)]
        total[d * pairs : (d + 1) * pairs] = block
        rows[d * pairs : (d + 1) * pairs] = block.astype(BF)
    for k in range(amps_ref.shape[1] // step):
        n, part = divmod(first + k * step, width)
        cols = pl.ds(k * step, step)
        prod = dot(rows[...], amps_ref[:, cols])
        prod += jnp.where(y == n, total[:, part : part + step], 0.0)
        own_ref[:, cols] = prod[:pairs]
        for d in range(1, NY):
            send_refs[d - 1][:, cols] = prod[d * pairs : (d + 1) * pairs].astype(send_refs[d - 1].dtype)


def out_products(place, total, amps_i, first, pairs, kept):
    rows, cols = amps_i.shape
    types = [F32 if d in (0, kept) else BF for d in range(NY)]
    return pl.pallas_call(
        functools.partial(out_kernel, pairs, first),
        out_shape=[jax.ShapeDtypeStruct((pairs, cols), t) for t in types],
        in_specs=[SMEM, VMEM, VMEM],
        out_specs=[VMEM] * NY,
        scratch_shapes=[
            pltpu.VMEM(total.shape, F32),
            pltpu.VMEM(total.shape, BF),
        ],
        compiler_params=params(10),
        cost_estimate=cost(2 * total.size * cols),
    )(place, total, amps_i)


def shards(pair_table, cholesky, amplitudes, denominators):
    y, z, x, c = (lax.axis_index(a) for a in ("y", "z", "x", "c"))
    place = jnp.stack([y, z, c])
    amps = amplitudes[0]
    pairs, naux = amps.shape[0], cholesky.shape[1]
    aux = -(-naux // (128 * NY)) * 128
    width = NZ * pairs
    rows = NY * pairs
    third = pairs // NX

    early = 4 * NY * width // 8
    amps_i0 = lax.all_gather(amps[:, :early], "z", axis=0, tiled=True)
    by_z = jnp.transpose(amps.reshape(pairs, NY, NZ, pairs), (0, 2, 1, 3)).reshape(pairs, NY * width)

    own = jnp.pad(jnp.transpose(cholesky[0]), ((0, 0), (0, NY * aux - naux)))
    own = jnp.transpose(own.reshape(NX, third, NY, aux), (0, 2, 1, 3)).reshape(NX * NY, third, aux)
    held = lax.all_to_all(own, ("x", "y"), split_axis=0, concat_axis=0, tiled=True).reshape(NX, NY, third, aux)
    sent, by_z = choose(swap_kernel, (held, by_z), place, pair_table, held, by_z)
    late = amps[:, early:]
    mine, later = choose(mine_kernel, (held, late), place, pair_table, held, shift(sent, "c", 1), late)
    amps_j = lax.all_gather(by_z, "y", axis=0, tiled=True)
    parts = lax.all_to_all(mine, "x", split_axis=0, concat_axis=0, tiled=True)
    chosen = after(join(parts).reshape(rows, aux), amps_i0)

    dist, blocks = [0], [chosen]
    fore = back = chosen
    for s in range(1, NZ // 2):
        fore, back = shift(fore, "z", 1), shift(back, "z", -1)
        dist += [-s, s]
        blocks += [fore, back]
    far_a, far_b = last_step(fore, back)
    far_a, far_b = shift(far_a, "z", 1), shift(far_b, "z", -1)
    amps_i1 = lax.all_gather(later, "z", axis=0, tiled=True)

    acc, full, amps_last = add_left(place, amps_j, dist, blocks)
    part, kept = (jax.ShapeDtypeStruct((rows, width // 2), t) for t in (BF, F32))
    left, two_a, two_b = pl.pallas_call(
        functools.partial(first_kernel, pairs),
        out_shape=[jax.ShapeDtypeStruct((rows, aux), BF), part, part],
        in_specs=[SMEM] + [VMEM] * 5,
        out_specs=[VMEM] * 3,
        compiler_params=params(8),
        cost_estimate=cost(2 * rows * aux * (rows + width)),
    )(place, amps_last, acc, full, far_a, far_b)
    one_a, one_b, three_a, three_b, own_a, own_b, amps_i0 = pl.pallas_call(
        functools.partial(second_kernel, pairs),
        out_shape=[kept, part, part, kept, kept, kept, jax.ShapeDtypeStruct(amps_i0.shape, BF)],
        in_specs=[SMEM] + [VMEM] * 4 + [ANY],
        out_specs=[VMEM] * 7,
        scratch_shapes=[pltpu.SemaphoreType.DMA],
        compiler_params=params(8),
        cost_estimate=cost(6 * rows * aux * width),
    )(place, left, full, far_a, far_b, amps_i0)
    relay_a, relay_b = shift(two_a, "y", 1), shift(two_b, "y", -1)
    direct_a, direct_b = shift(three_a, "y", -1), shift(one_b, "y", 1)
    direct = jnp.concatenate([direct_a, direct_b], axis=1).astype(F32)
    relay_a = shift((one_a + relay_a.astype(F32)).astype(BF), "y", 1)
    relay_b = shift((three_b + relay_b.astype(F32)).astype(BF), "y", -1)
    own = jnp.concatenate([own_a, own_b], axis=1)
    total = own + direct + jnp.concatenate([relay_a, relay_b], axis=1).astype(F32)

    own_a, one_a, two_a, three_a = out_products(place, total, amps_i0, 0, pairs, 1)
    relay_a, direct_a = shift(two_a, "y", 1), shift(three_a, "y", -1)
    own_b, one_b, two_b, three_b = out_products(place, total, amps_i1, early, pairs, 3)
    relay_b, direct_b = shift(two_b, "y", -1), shift(one_b, "y", 1)
    own = jnp.concatenate([own_a, own_b], axis=1)
    direct = jnp.concatenate([direct_a, direct_b], axis=1).astype(F32)
    relay_a = shift((one_a + relay_a.astype(F32)).astype(BF), "y", 1)
    relay_b = shift((three_b + relay_b.astype(F32)).astype(BF), "y", -1)
    out = own + direct + jnp.concatenate([relay_a, relay_b], axis=1).astype(F32)
    return (-out / denominators[0]).astype(BF)[None]


def solution(mesh):
    grid = Mesh(mesh.devices.reshape(NY, NZ, NX, NC), ("y", "z", "x", "c"))
    ka, row = ("x", "c"), ("y", "z")
    in_specs = (P(), P(ka, None, row), P(ka, row, None), P(ka, row, None))
    return jax.shard_map(shards, mesh=grid, in_specs=in_specs, out_specs=P(ka, row, None), check_vma=False)
```
